32 devices in a mesh: dp: 8 (over z, x), fsdp: 4 (over y, core).
Axes of the slice: x: 2, y: 2, z: 4, core: 2. Of those that a mesh axis runs over, the one named last changes fastest.
Arguments:
- inputs: bfloat16 [16, 1024, 1024], P('dp', 'fsdp'), may hold values from -6 to 6
- segment_ids: int32 [16, 1024], P('dp', 'fsdp'), may hold values from 0 to 2, as said below
- cotangent: bfloat16 [16, 1024, 1024], P('dp', 'fsdp'), may hold values from -6 to 6
- ln1_gain: bfloat16 [1024], P(('dp', 'fsdp')), may hold values from 0.5 to 1.5
- ln1_bias: bfloat16 [1024], P(('dp', 'fsdp')), may hold values from -1.75 to 1.75
- w_qkv: bfloat16 [1024, 3072], P(('dp', 'fsdp')), may hold values from -0.1875 to 0.1875
- q_bias: bfloat16 [1024], P(('dp', 'fsdp')), may hold values from -3 to 3
- v_bias: bfloat16 [1024], P(('dp', 'fsdp')), may hold values from -3 to 3
- w_proj: bfloat16 [1024, 1024], P(('dp', 'fsdp')), may hold values from -2 to 2
- proj_bias: bfloat16 [1024], P(('dp', 'fsdp')), may hold values from -1.75 to 1.75
- ln2_gain: bfloat16 [1024], P(('dp', 'fsdp')), may hold values from 0.5 to 1.5
- ln2_bias: bfloat16 [1024], P(('dp', 'fsdp')), may hold values from -1.75 to 1.75
- w_fc: bfloat16 [1024, 4096], P(('dp', 'fsdp')), may hold values from -0.1875 to 0.1875
- fc_bias: bfloat16 [4096], P(('dp', 'fsdp')), may hold values from -3 to 3
- w_out: bfloat16 [4096, 1024], P(('dp', 'fsdp')), may hold values from -0.09375 to 0.09375
- out_bias: bfloat16 [1024], P(('dp', 'fsdp')), may hold values from -1.75 to 1.75
Outputs:
- block_output: bfloat16 [16, 1024, 1024], P('dp', 'fsdp')
- input_grad: bfloat16 [16, 1024, 1024], P('dp', 'fsdp')
- ln1_gain_grad: float32 [1024], P(('dp', 'fsdp'))
- ln1_bias_grad: float32 [1024], P(('dp', 'fsdp'))
- w_qkv_grad: float32 [1024, 3072], P(('dp', 'fsdp'))
- q_bias_grad: float32 [1024], P(('dp', 'fsdp'))
- v_bias_grad: float32 [1024], P(('dp', 'fsdp'))
- w_proj_grad: float32 [1024, 1024], P(('dp', 'fsdp'))
- proj_bias_grad: float32 [1024], P(('dp', 'fsdp'))
- ln2_gain_grad: float32 [1024], P(('dp', 'fsdp'))
- ln2_bias_grad: float32 [1024], P(('dp', 'fsdp'))
- w_fc_grad: float32 [1024, 4096], P(('dp', 'fsdp'))
- fc_bias_grad: float32 [4096], P(('dp', 'fsdp'))
- w_out_grad: float32 [4096, 1024], P(('dp', 'fsdp'))
- out_bias_grad: float32 [1024], P(('dp', 'fsdp'))
The draws below stay inside these ranges and needn't reach their ends.
Inputs may be any that keep to these rules, and one draw needn't show every extreme that they name: `segment_ids`: within each sequence the ids start at 0 and never fall; every sequence that holds several documents ends with document 2; among the 2 sequences of each dp index one is a single document.
All inputs are finite; a program needn't handle non-finite values.
Results may differ from the reference program's by a relative error of at most 0.013.
Values may be sent and summed in bfloat16 or wider, within the bound.
A program may use at most 192 MiB of HBM per device.

```python
import jax
import jax.numpy as jnp
from jax import lax

D = 1024
FF = 4096
H = 16
HD = 64
SEQ_LEN = 1024
SEQS_DEV = 2
SEQS = 16


def draw_segment_ids(key, part):
    key = jax.random.fold_in(key, 7)
    key_len, key_start, key_pick = jax.random.split(key, 3)
    lengths = jax.random.randint(key_len, (SEQS, 8), SEQ_LEN // 5, SEQ_LEN // 3 + 1)
    offset = jax.random.randint(key_start, (SEQS, 1), 0, SEQ_LEN // 5)
    ends = jnp.cumsum(lengths, axis=1) - offset
    positions = jnp.arange(SEQ_LEN)
    doc_ids = jnp.sum((positions[None, :, None] >= ends[:, None, :]).astype(jnp.int32), axis=2)
    doc_ids = jnp.minimum(doc_ids, 2)
    chosen = jax.random.randint(key_pick, (SEQS // SEQS_DEV, 1), 0, SEQS_DEV)
    single = (jnp.arange(SEQS).reshape(SEQS // SEQS_DEV, SEQS_DEV) == chosen).reshape(SEQS)
    return jnp.where(single[:, None], 0, doc_ids).astype(jnp.int32)


def block_scale(key, shape, shards, smallest, largest):
    level, own = 1.0, jax.random.fold_in(key, 6)
    for position, parts in shards:
        steps = jnp.exp(jax.random.uniform(jax.random.fold_in(own, position), (parts,), jnp.float32, smallest / len(shards), largest / len(shards)))
        level = level * jnp.repeat(steps, shape[position] // parts).reshape([-1 if axis == position else 1 for axis in range(len(shape))])
    return level


def centred(stream_key, dims, deviation, limit, pieces=(), dtype=jnp.bfloat16):
    level = block_scale(stream_key, dims, pieces, -0.22, 0.18) if pieces else 1.0
    array = jax.random.normal(stream_key, dims, jnp.float32) * deviation * level
    return jnp.minimum(jnp.maximum(array, -limit), limit).astype(dtype)


def setup_inputs(seed: int = 0) -> dict:
    streams_of = jax.random.split(jax.random.key(seed), 17)
    return {
        "inputs": centred(streams_of[0], (SEQS, SEQ_LEN, D), 1.0, 6.0, ((0, 8), (1, 4))),
        "segment_ids": draw_segment_ids(jax.random.fold_in(streams_of[16], 71), 0),
        "cotangent": centred(streams_of[2], (SEQS, SEQ_LEN, D), 1.0, 6.0, ((0, 8), (1, 4))),
        "ln1_gain": jnp.clip(1.0 + 0.1 * jax.random.normal(streams_of[3], (D,), jnp.float32), 0.5, 1.5).astype(jnp.bfloat16),
        "ln1_bias": centred(streams_of[4], (D,), 0.3, 1.75, ((0, 32),)),
        "w_qkv": centred(streams_of[5], (D, 3 * D), D ** -0.5, 0.1875, ((0, 32),)),
        "q_bias": centred(streams_of[6], (D,), 0.5, 3.0, ((0, 32),)),
        "v_bias": centred(streams_of[7], (D,), 0.5, 3.0, ((0, 32),)),
        "w_proj": centred(streams_of[8], (D, D), (D // 128) ** -0.5, 2.0, ((0, 32),)),
        "proj_bias": centred(streams_of[9], (D,), 0.3, 1.75, ((0, 32),)),
        "ln2_gain": jnp.clip(1.0 + 0.1 * jax.random.normal(streams_of[10], (D,), jnp.float32), 0.5, 1.5).astype(jnp.bfloat16),
        "ln2_bias": centred(streams_of[11], (D,), 0.3, 1.75, ((0, 32),)),
        "w_fc": centred(streams_of[12], (D, FF), D ** -0.5, 0.1875, ((0, 32),)),
        "fc_bias": centred(streams_of[13], (FF,), 0.5, 3.0, ((0, 32),)),
        "w_out": centred(streams_of[14], (FF, D), FF ** -0.5, 0.09375, ((0, 32),)),
        "out_bias": centred(streams_of[15], (D,), 0.3, 1.75, ((0, 32),)),
    }


@jax.custom_vjp
def low(v):
    return lax.optimization_barrier(v.astype(jnp.bfloat16)).astype(jnp.float32)

@jax.custom_vjp
def low_back(v):
    return v

def low_keep(v):
    return (low(v), None)

def low_pass(kept, grad):
    return (grad,)

def back_keep(v):
    return (v, None)

def back_low(kept, grad):
    return (low(grad),)
low.defvjp(low_keep, low_pass)
low_back.defvjp(back_keep, back_low)

def matmul(left, right):
    return jnp.dot(left, right, precision=lax.Precision.HIGHEST)

def layer_norm(values, gain, shift):
    center = values - lax.optimization_barrier(jnp.mean(values, axis=-1, keepdims=True))
    spread = lax.optimization_barrier(jnp.mean(center * center, axis=-1, keepdims=True))
    return center * lax.rsqrt(spread + 1e-05) * gain + shift

def attend(item):
    query, keys, values, segment = item
    positions = jnp.arange(SEQ_LEN)
    allowed = (segment[:, None] == segment[None, :]) & (positions[None, :] <= positions[:, None])
    query = query.reshape(SEQ_LEN, H, HD)
    keys = keys.reshape(SEQ_LEN, H, HD)
    values = values.reshape(SEQ_LEN, H, HD)
    scores = low_back(jnp.einsum('qhd,khd->hqk', query, keys, precision=lax.Precision.HIGHEST) * HD ** (-0.5))
    scores = jnp.where(allowed[None], scores, -1e+30)
    weights = low(jax.nn.softmax(scores, axis=-1))
    mixed = jnp.einsum('hqk,khd->qhd', weights, values, precision=lax.Precision.HIGHEST)
    return mixed.reshape(SEQ_LEN, D)

def forward(tokens, segments, params):
    ln1_gain, ln1_bias, w_qkv, q_bias, v_bias, w_proj, proj_bias, ln2_gain, ln2_bias, w_fc, fc_bias, w_out, out_bias = params
    normed = low(layer_norm(tokens, ln1_gain, ln1_bias))
    bias_all = jnp.concatenate([q_bias, jnp.zeros_like(q_bias), v_bias])
    projected = low(low_back(matmul(normed, w_qkv) + bias_all))
    query, keys, values = jnp.split(projected, 3, axis=-1)
    mixed = lax.map(jax.checkpoint(attend), (query, keys, values, segments))
    mixed = low(low_back(mixed))
    middle = tokens + low_back(matmul(mixed, w_proj) + proj_bias)
    normed_two = low(layer_norm(middle, ln2_gain, ln2_bias))
    hidden = low_back(matmul(normed_two, w_fc) + fc_bias)
    active = low(jax.nn.gelu(hidden, approximate=True))
    return middle + low_back(matmul(active, w_out) + out_bias)

def reference(inputs, segment_ids, cotangent, ln1_gain, ln1_bias, w_qkv, q_bias, v_bias, w_proj, proj_bias, ln2_gain, ln2_bias, w_fc, fc_bias, w_out, out_bias):
    params = tuple((item.astype(jnp.float32) for item in (ln1_gain, ln1_bias, w_qkv, q_bias, v_bias, w_proj, proj_bias, ln2_gain, ln2_bias, w_fc, fc_bias, w_out, out_bias)))
    groups = SEQS // 4
    token_groups = inputs.astype(jnp.float32).reshape(groups, 4, SEQ_LEN, D)
    segment_groups = segment_ids.astype(jnp.int32).reshape(groups, 4, SEQ_LEN)
    cot_groups = cotangent.astype(jnp.float32).reshape(groups, 4, SEQ_LEN, D)

    def step(totals, item):
        tokens, segments, cot_part = item
        result, back_fn = jax.vjp(lambda first, *rest: forward(first, segments, rest), tokens, *params)
        grads = back_fn(cot_part)
        totals = tuple((left + right for left, right in zip(totals, grads[1:])))
        return (totals, (result.astype(jnp.bfloat16), grads[0].astype(jnp.bfloat16)))
    start = tuple((jnp.zeros(item.shape, jnp.float32) for item in params))
    totals, (results, input_grads) = lax.scan(step, start, (token_groups, segment_groups, cot_groups))
    return (results.reshape(SEQS, SEQ_LEN, D), input_grads.reshape(SEQS, SEQ_LEN, D), totals[0], totals[1], totals[2], totals[3], totals[4], totals[5], totals[6], totals[7], totals[8], totals[9], totals[10], totals[11], totals[12])
```

```python
import jax
import jax.numpy as jnp
from jax import lax
from jax.sharding import PartitionSpec as P

H = 16
HD = 64
PERMUTE = True


def layer_norm(values, gain, shift):
    center = values - jnp.mean(values, axis=-1, keepdims=True)
    spread = jnp.mean(center * center, axis=-1, keepdims=True)
    return center * lax.rsqrt(spread + 1e-05) * gain + shift


def gelu_tanh(values):
    return jax.nn.gelu(values, approximate=True)


def row_dot(left, right):
    return jnp.dot(left, right, preferred_element_type=jnp.float32)


def col_dot(left, right):
    return lax.dot_general(
        left, right, (((0,), (0,)), ((), ())), preferred_element_type=jnp.float32
    )


def back_dot(left, right):
    return lax.dot_general(
        left, right, (((1,), (1,)), ((), ())), preferred_element_type=jnp.float32
    )


def score_block(queries, keys_all, allowed):
    raw = jnp.einsum(
        "qhd,khd->hqk",
        queries.reshape(-1, H, HD),
        keys_all.reshape(-1, H, HD),
        preferred_element_type=jnp.float32,
    ) * HD ** (-0.5)
    return jnp.where(allowed[None], raw, -1e30)


def attend_forward(item):
    queries, keys_all, values_all, allowed = item
    scores = score_block(queries, keys_all, allowed)
    top_score = jnp.max(scores, axis=-1, keepdims=True)
    expon = jnp.exp(scores - top_score)
    total = jnp.sum(expon, axis=-1, keepdims=True)
    weights = (expon / total).astype(jnp.bfloat16)
    mixed = jnp.einsum(
        "hqk,khd->qhd", weights, values_all.reshape(-1, H, HD), preferred_element_type=jnp.float32
    )
    return (mixed.reshape(queries.shape[0], H * HD), top_score[..., 0] + jnp.log(total[..., 0]))


def attend_backward(item):
    queries, keys_all, values_all, allowed, grad_mixed, log_total = item
    scores = score_block(queries, keys_all, allowed)
    probs = jnp.exp(scores - log_total[:, :, None])
    weights = probs.astype(jnp.bfloat16)
    grad_heads = grad_mixed.reshape(-1, H, HD)
    key_heads = keys_all.reshape(-1, H, HD)
    grad_weights = jnp.einsum(
        "qhd,khd->hqk",
        grad_heads,
        values_all.reshape(-1, H, HD),
        preferred_element_type=jnp.float32,
    )
    inner = jnp.sum(probs * grad_weights, axis=-1, keepdims=True)
    grad_scores = (probs * (grad_weights - inner)).astype(jnp.bfloat16)
    grad_query = jnp.einsum(
        "hqk,khd->qhd", grad_scores, key_heads, preferred_element_type=jnp.float32
    ) * HD ** (-0.5)
    grad_key = jnp.einsum(
        "hqk,qhd->khd", grad_scores, queries.reshape(-1, H, HD), preferred_element_type=jnp.float32
    ) * HD ** (-0.5)
    grad_value = jnp.einsum("hqk,qhd->khd", weights, grad_heads, preferred_element_type=jnp.float32)
    return (
        grad_query.reshape(queries.shape[0], H * HD),
        grad_key.reshape(keys_all.shape[0], H * HD),
        grad_value.reshape(keys_all.shape[0], H * HD),
    )


def share_pack(segment_ids, vectors):
    batch, local_len = segment_ids.shape
    flat = jnp.concatenate([item for item in vectors] + [segment_ids.astype(jnp.bfloat16).reshape(-1)])
    rows = -(-flat.shape[0] // 2048) * 16
    flat = jnp.pad(flat, (0, rows * 128 - flat.shape[0])).reshape(rows, 128)
    everyone = lax.all_gather(flat, ("dp", "fsdp"), axis=0, tiled=True)
    everyone = everyone.reshape(-1, rows * 128)
    out = []
    low = 0
    for item in vectors:
        out.append(everyone[:, low : low + item.shape[0]].reshape(-1))
        low += item.shape[0]
    ranks = lax.axis_size("fsdp")
    mine = lax.dynamic_slice_in_dim(everyone, lax.axis_index("dp") * ranks, ranks, axis=0)
    mine = mine[:, low : low + batch * local_len].reshape(ranks, batch, local_len)
    key_segments = mine.transpose(1, 0, 2).reshape(batch, ranks * local_len).astype(jnp.int32)
    return out, key_segments


def scatter_pack(vectors):
    shards = lax.axis_size(("dp", "fsdp"))
    parts = [item.reshape(shards, -1) for item in vectors]
    flat = jnp.concatenate(parts, axis=1)
    rows = -(-flat.shape[1] // 1024) * 8
    flat = jnp.pad(flat, ((0, 0), (0, rows * 128 - flat.shape[1]))).reshape(shards * rows, 128)
    owned = lax.psum_scatter(flat, ("dp", "fsdp"), scatter_dimension=0, tiled=True).reshape(-1)
    out = []
    low = 0
    for item in parts:
        out.append(owned[low : low + item.shape[1]])
        low += item.shape[1]
    return out


def scatter_low(total):
    return lax.psum_scatter(
        total.astype(jnp.bfloat16), ("dp", "fsdp"), scatter_dimension=0, tiled=True
    ).astype(jnp.float32)


def share_keys(own):
    ranks = lax.axis_size("fsdp")
    if ranks != 4 or not PERMUTE:
        return lax.all_gather(own, "fsdp", axis=1, tiled=True)
    rank = lax.axis_index("fsdp")
    far = lax.ppermute(own, "fsdp", [(0, 2), (1, 3)])
    near = lax.ppermute(own, "fsdp", [(0, 1), (1, 0), (2, 3), (3, 2)])
    far_near = lax.ppermute(far, "fsdp", [(2, 3), (3, 2)])
    odd = (rank % 2) == 1
    high = rank >= 2
    pair = [jnp.where(odd, near, own), jnp.where(odd, own, near)]
    far_pair = [jnp.where(odd, far_near, far), jnp.where(odd, far, far_near)]
    empty = jnp.zeros_like(own)
    return jnp.concatenate(
        [
            jnp.where(high, far_pair[0], pair[0]),
            jnp.where(high, far_pair[1], pair[1]),
            jnp.where(high, pair[0], empty),
            jnp.where(high, pair[1], empty),
        ],
        axis=1,
    )


def return_keys(terms):
    ranks = lax.axis_size("fsdp")
    if ranks != 4 or not PERMUTE:
        return lax.psum_scatter(
            terms.astype(jnp.bfloat16), "fsdp", scatter_dimension=1, tiled=True
        ).astype(jnp.float32)
    rank = lax.axis_index("fsdp")
    part = terms.shape[1] // 4
    low_terms = terms.astype(jnp.bfloat16)
    odd = rank % 2
    other = 1 - odd
    base = (rank // 2) * 2
    pairs = [(0, 1), (1, 0), (2, 3), (3, 2)]

    def block(array, index):
        return lax.dynamic_slice_in_dim(array, index * part, part, axis=1)

    first = lax.ppermute(block(low_terms, other), "fsdp", [(2, 3), (3, 2)])
    far_sum = block(terms, odd) + first.astype(jnp.float32)
    near = lax.ppermute(block(low_terms, base + other), "fsdp", pairs)
    far = lax.ppermute(far_sum.astype(jnp.bfloat16), "fsdp", [(2, 0), (3, 1)])
    return block(terms, base + odd) + near.astype(jnp.float32) + far.astype(jnp.float32)


def on_device(
    inputs,
    segment_ids,
    cotangent,
    ln1_gain,
    ln1_bias,
    w_qkv,
    q_bias,
    v_bias,
    w_proj,
    proj_bias,
    ln2_gain,
    ln2_bias,
    w_fc,
    fc_bias,
    w_out,
    out_bias,
):
    batch, local_len, width = inputs.shape
    rank = lax.axis_index("fsdp")
    full_len = local_len * lax.axis_size("fsdp")
    small, key_segments = share_pack(
        segment_ids,
        (ln1_gain, ln1_bias, q_bias, v_bias, proj_bias, ln2_gain, ln2_bias, fc_bias, out_bias),
    )
    (
        gain_first,
        shift_first,
        query_shift,
        value_shift,
        proj_shift,
        gain_second,
        shift_second,
        expand_shift,
        shrink_shift,
    ) = [item.astype(jnp.float32) for item in small]
    qkv_full = lax.all_gather(w_qkv, ("dp", "fsdp"), axis=0, tiled=True)
    proj_full = lax.all_gather(w_proj, ("dp", "fsdp"), axis=0, tiled=True)
    expand_full = lax.all_gather(w_fc, ("dp", "fsdp"), axis=0, tiled=True)
    shrink_full = lax.all_gather(w_out, ("dp", "fsdp"), axis=0, tiled=True)
    query_pos = rank * local_len + jnp.arange(local_len)
    key_pos = jnp.arange(full_len)
    causal = key_pos[None, :] <= query_pos[:, None]
    allowed = (segment_ids[:, :, None] == key_segments[:, None, :]) & causal[None]

    tokens_in = inputs.astype(jnp.float32).reshape(-1, width)
    normed_low = layer_norm(tokens_in, gain_first, shift_first).astype(jnp.bfloat16)
    bias_all = jnp.concatenate([query_shift, jnp.zeros_like(query_shift), value_shift])
    projected = (
        (row_dot(normed_low, qkv_full) + bias_all)
        .astype(jnp.bfloat16)
        .reshape(batch, local_len, 3 * width)
    )
    queries = projected[:, :, :width]
    both_all = share_keys(projected[:, :, width:])
    keys_all = both_all[:, :, :width]
    values_all = both_all[:, :, width:]
    mixed, log_total = lax.map(attend_forward, (queries, keys_all, values_all, allowed))
    mixed_low = mixed.astype(jnp.bfloat16).reshape(-1, width)
    middle = tokens_in + row_dot(mixed_low, proj_full) + proj_shift
    normed_two_low = layer_norm(middle, gain_second, shift_second).astype(jnp.bfloat16)
    hidden = row_dot(normed_two_low, expand_full) + expand_shift
    active_low = gelu_tanh(hidden).astype(jnp.bfloat16)
    result = middle + row_dot(active_low, shrink_full) + shrink_shift
    block_output = result.astype(jnp.bfloat16).reshape(batch, local_len, width)

    grad_branch = cotangent.reshape(-1, width)
    grad_out = grad_branch.astype(jnp.float32)
    out_bias_grad = jnp.sum(grad_out, axis=0)
    w_out_grad = scatter_low(col_dot(active_low, grad_branch))
    grad_active = back_dot(grad_branch, shrink_full)
    _, gelu_back = jax.vjp(gelu_tanh, hidden)
    grad_hidden = gelu_back(grad_active)[0].astype(jnp.bfloat16)
    fc_bias_grad = jnp.sum(grad_hidden.astype(jnp.float32), axis=0)
    w_fc_grad = scatter_low(col_dot(normed_two_low, grad_hidden))
    grad_normed_two = back_dot(grad_hidden, expand_full)
    _, second_back = jax.vjp(layer_norm, middle, gain_second, shift_second)
    grad_mid_part, grad_gain_two, grad_shift_two = second_back(grad_normed_two)
    grad_middle = grad_out + grad_mid_part
    grad_mid_low = grad_middle.astype(jnp.bfloat16)
    proj_bias_grad = jnp.sum(grad_mid_low.astype(jnp.float32), axis=0)
    w_proj_grad = scatter_low(col_dot(mixed_low, grad_mid_low))
    grad_mixed = (
        back_dot(grad_mid_low, proj_full).astype(jnp.bfloat16).reshape(batch, local_len, width)
    )
    grad_query, key_terms, value_terms = lax.map(
        attend_backward, (queries, keys_all, values_all, allowed, grad_mixed, log_total)
    )
    grad_both = return_keys(jnp.concatenate([key_terms, value_terms], axis=-1))
    grad_projected = (
        jnp.concatenate([grad_query, grad_both], axis=-1)
        .astype(jnp.bfloat16)
        .reshape(-1, 3 * width)
    )
    q_bias_grad = jnp.sum(grad_projected[:, :width].astype(jnp.float32), axis=0)
    v_bias_grad = jnp.sum(grad_projected[:, 2 * width :].astype(jnp.float32), axis=0)
    w_qkv_grad = scatter_low(col_dot(normed_low, grad_projected))
    grad_normed = back_dot(grad_projected, qkv_full)
    _, first_back = jax.vjp(layer_norm, tokens_in, gain_first, shift_first)
    grad_in_part, grad_gain_one, grad_shift_one = first_back(grad_normed)
    input_grad = (grad_middle + grad_in_part).astype(jnp.bfloat16).reshape(batch, local_len, width)
    owned = scatter_pack(
        (
            grad_gain_one,
            grad_shift_one,
            q_bias_grad,
            v_bias_grad,
            proj_bias_grad,
            grad_gain_two,
            grad_shift_two,
            fc_bias_grad,
            out_bias_grad,
        )
    )
    return (
        block_output,
        input_grad,
        owned[0],
        owned[1],
        w_qkv_grad,
        owned[2],
        owned[3],
        w_proj_grad,
        owned[4],
        owned[5],
        owned[6],
        w_fc_grad,
        owned[7],
        w_out_grad,
        owned[8],
    )


def solution(mesh):
    placed = (
        P("dp", "fsdp", None),
        P("dp", "fsdp"),
        P("dp", "fsdp", None),
        P(("dp", "fsdp")),
        P(("dp", "fsdp")),
        P(("dp", "fsdp"), None),
        P(("dp", "fsdp")),
        P(("dp", "fsdp")),
        P(("dp", "fsdp"), None),
        P(("dp", "fsdp")),
        P(("dp", "fsdp")),
        P(("dp", "fsdp")),
        P(("dp", "fsdp"), None),
        P(("dp", "fsdp")),
        P(("dp", "fsdp"), None),
        P(("dp", "fsdp")),
    )
    return jax.shard_map(
        on_device,
        mesh=mesh,
        in_specs=placed,
        out_specs=(
            P("dp", "fsdp", None),
            P("dp", "fsdp", None),
            P(("dp", "fsdp")),
            P(("dp", "fsdp")),
            P(("dp", "fsdp"), None),
            P(("dp", "fsdp")),
            P(("dp", "fsdp")),
            P(("dp", "fsdp"), None),
            P(("dp", "fsdp")),
            P(("dp", "fsdp")),
            P(("dp", "fsdp")),
            P(("dp", "fsdp"), None),
            P(("dp", "fsdp")),
            P(("dp", "fsdp"), None),
            P(("dp", "fsdp")),
        ),
        check_vma=False,
    )
```
